256 devices in a mesh: ctx: 64 (over y_hi, z, x), head: 4 (over y_lo, core).
Axes of the slice: x: 4, y: 4 (y_hi: 2, y_lo: 2; y = y_hi * 2 + y_lo), z: 8, core: 2. Of those that a mesh axis runs over, the one named last changes fastest.
Arguments:
- queries: bfloat16 [32768, 2560], P(('ctx', 'head')), may hold values from -6 to 6
- keys: bfloat16 [32768, 512], P(('ctx', 'head')), may hold values from -6 to 6
- values: bfloat16 [32768, 512], P(('ctx', 'head')), may hold values from -6 to 6
- attn_out: bfloat16 [32768, 2560], P(('ctx', 'head')), may hold values from -6 to 6
- grad_out: bfloat16 [32768, 2560], P(('ctx', 'head')), may hold values from -6 to 6
- log_norm: float32 [20, 32768], P(None, ('ctx', 'head'))
- doc_lengths: int32 [64], replicated, may hold values from 1 to 3072, as said below
Outputs:
- grad_queries: bfloat16 [32768, 2560], P(('ctx', 'head'))
- grad_keys: bfloat16 [32768, 512], P(('ctx', 'head'))
- grad_values: bfloat16 [32768, 512], P(('ctx', 'head'))
The draws below stay inside these ranges and needn't reach their ends.
Inputs may be any that keep to these rules, and one draw needn't show every extreme that they name: `doc_lengths`: 64 lengths that sum to 32768; the first document has fewer than 512 tokens and the second has 3072.
All inputs are finite; a program needn't handle non-finite values.
Results may differ from the reference program's by a relative error of at most 0.0054.
Values may be sent and summed in bfloat16 or wider, within the bound.
A program may use at most 64 MiB of HBM per device.

```python
import jax
import jax.numpy as jnp
from jax import lax

QH = 20
KVH = 4
HD = 128
TOK_DEV = 512
TOKENS = 32768
MOST = 3072
DOCS = 64


def length_table(key):
    first_key, long_key, weight_key, place_key = jax.random.split(key, 4)
    extra_count = min(3, max(0, (TOKENS - MOST - TOK_DEV - 2 * DOCS) // MOST))
    others = DOCS - 2 - extra_count
    first_doc = jax.random.randint(first_key, (1,), 1, TOK_DEV).astype(jnp.int32)
    if extra_count > 0:
        long_docs = (MOST - jax.random.randint(long_key, (extra_count,), 0, TOK_DEV)).astype(jnp.int32)
    else:
        long_docs = jnp.zeros((0,), jnp.int32)
    rest_tokens = (TOKENS - MOST - jnp.sum(first_doc) - jnp.sum(long_docs)).astype(jnp.int32)
    spare_tokens = rest_tokens - others
    shares = jax.random.randint(weight_key, (others,), 1, 9).astype(jnp.int32)
    short_docs = 1 + shares * spare_tokens // jnp.sum(shares)
    missing = rest_tokens - jnp.sum(short_docs)
    short_docs = short_docs + (jnp.arange(others, dtype=jnp.int32) < missing).astype(jnp.int32)
    mixed_docs = jax.random.permutation(place_key, jnp.concatenate([long_docs, short_docs.astype(jnp.int32)]))
    length_rows = jnp.concatenate([first_doc, jnp.full((1,), MOST, jnp.int32), mixed_docs.astype(jnp.int32)])
    return length_rows.astype(jnp.int32)


def draw_doc_lengths(key, part):
    return length_table(key)


def draw_log_norm(key, part):
    lengths = length_table(key)
    key = jax.random.fold_in(key, 7)
    doc_ends = jnp.cumsum(lengths).astype(jnp.int32)
    positions = jnp.arange(TOKENS, dtype=jnp.int32)
    starts = jnp.max(jnp.where(doc_ends[None, :] <= positions[:, None], doc_ends[None, :], 0), axis=1)
    visible = (positions - starts + 1).astype(jnp.float32)
    center = jnp.log(visible) + 0.5
    noise = jnp.clip(0.4 * jax.random.normal(key, (QH, TOKENS), jnp.float32), -0.8, 0.8)
    return (center[None, :] + noise).astype(jnp.float32)


def steps_of(stream_key, dims, cuts, low, high):
    def one(position, shards_of):
        heights = jax.random.uniform(jax.random.fold_in(jax.random.fold_in(stream_key, 6), position), (shards_of,), jnp.float32, low / len(cuts), high / len(cuts))
        return jnp.repeat(jnp.exp(heights), dims[position] // shards_of).reshape((-1,) + (1,) * (len(dims) - position - 1))

    factor_of = one(*cuts[0])
    for cut in cuts[1:]:
        factor_of = factor_of * one(*cut)
    return factor_of


def bell_draw(key, shape, spread, bound, pieces=(), kind=jnp.bfloat16):
    values = jax.random.normal(key, shape, jnp.float32) * spread
    if len(pieces) > 0:
        values = steps_of(key, shape, pieces, -0.22, 0.18) * values
    return jnp.clip(values, min=-bound, max=bound).astype(kind)


def setup_inputs(seed: int = 0) -> dict:
    splits = jax.random.split(jax.random.key(seed), 8)
    return {
        "queries": bell_draw(splits[0], (TOKENS, QH * HD), 1.0, 6.0, ((0, 256),)),
        "keys": bell_draw(splits[1], (TOKENS, KVH * HD), 1.0, 6.0, ((0, 256),)),
        "values": bell_draw(splits[2], (TOKENS, KVH * HD), 1.0, 6.0, ((0, 256),)),
        "attn_out": bell_draw(splits[3], (TOKENS, QH * HD), 1.0, 6.0, ((0, 256),)),
        "grad_out": bell_draw(splits[4], (TOKENS, QH * HD), 1.0, 6.0, ((0, 256),)),
        "log_norm": draw_log_norm(jax.random.fold_in(splits[7], 71), 0),
        "doc_lengths": draw_doc_lengths(jax.random.fold_in(splits[7], 71), 0),
    }


def doc_starts(positions, doc_lengths):
    doc_ends = jnp.cumsum(doc_lengths).astype(jnp.int32)
    marked = jnp.where(doc_ends[None, :] <= positions[:, None], doc_ends[None, :], 0)
    return jnp.max(marked, axis=1).astype(jnp.int32)


def reference(queries, keys, values, attn_out, grad_out, log_norm, doc_lengths):
    group_size = QH // KVH
    softmax_scale = HD ** -0.5
    block_rows = 256 if TOKENS % 256 == 0 else TOKENS
    block_count = TOKENS // block_rows
    query_all = queries.reshape(TOKENS, KVH, group_size, HD)
    grad_all = grad_out.reshape(TOKENS, KVH, group_size, HD)
    key_all = keys.reshape(TOKENS, KVH, HD)
    value_all = values.reshape(TOKENS, KVH, HD)
    products = (grad_out.astype(jnp.float32) * attn_out.astype(jnp.float32)).reshape(TOKENS, QH, HD)
    delta_all = jnp.sum(products, axis=2).T.reshape(KVH, group_size, TOKENS)
    norm_all = log_norm.reshape(KVH, group_size, TOKENS)
    positions = jnp.arange(TOKENS, dtype=jnp.int32)
    row_starts = doc_starts(positions, doc_lengths)
    block_ids = jnp.arange(block_count, dtype=jnp.int32)

    def query_step(outer_state, block_index):
        key_grads, value_grads = outer_state
        query_first = block_index * block_rows
        query_block = lax.dynamic_slice_in_dim(query_all, query_first, block_rows, 0)
        grad_block = lax.dynamic_slice_in_dim(grad_all, query_first, block_rows, 0)
        norm_block = lax.dynamic_slice_in_dim(norm_all, query_first, block_rows, 2)
        delta_block = lax.dynamic_slice_in_dim(delta_all, query_first, block_rows, 2)
        query_places = lax.dynamic_slice_in_dim(positions, query_first, block_rows, 0)
        start_block = lax.dynamic_slice_in_dim(row_starts, query_first, block_rows, 0)

        def key_step(inner_state, key_index):
            query_grad, key_grads, value_grads = inner_state
            key_first = key_index * block_rows
            key_block = lax.dynamic_slice_in_dim(key_all, key_first, block_rows, 0)
            value_block = lax.dynamic_slice_in_dim(value_all, key_first, block_rows, 0)
            live_tile = (key_first <= query_first + block_rows - 1) & (key_first + block_rows - 1 >= start_block[0])

            def compute():
                key_places = key_first + jnp.arange(block_rows, dtype=jnp.int32)
                allowed = (key_places[None, :] >= start_block[:, None]) & (key_places[None, :] <= query_places[:, None])
                scores = jnp.einsum("igxd,jgd->gxij", query_block.astype(jnp.float32), key_block.astype(jnp.float32)) * softmax_scale
                weights = jnp.where(allowed[None, None], jnp.exp(scores - norm_block[..., None]), 0.0)
                weight_grads = jnp.einsum("igxd,jgd->gxij", grad_block.astype(jnp.float32), value_block.astype(jnp.float32))
                score_grads = weights * (weight_grads - delta_block[..., None])
                weights_low = weights.astype(jnp.bfloat16).astype(jnp.float32)
                grads_low = score_grads.astype(jnp.bfloat16).astype(jnp.float32)
                grad_query = jnp.einsum("gxij,jgd->igxd", grads_low, key_block.astype(jnp.float32)) * softmax_scale
                grad_key = jnp.einsum("gxij,igxd->jgd", grads_low, query_block.astype(jnp.float32)) * softmax_scale
                grad_value = jnp.einsum("gxij,igxd->jgd", weights_low, grad_block.astype(jnp.float32))
                return grad_query, grad_key, grad_value

            def skip():
                return (jnp.zeros((block_rows, KVH, group_size, HD), jnp.float32),
                        jnp.zeros((block_rows, KVH, HD), jnp.float32),
                        jnp.zeros((block_rows, KVH, HD), jnp.float32))

            grad_query, grad_key, grad_value = lax.cond(live_tile, compute, skip)
            old_key = lax.dynamic_slice_in_dim(key_grads, key_first, block_rows, 0)
            key_grads = lax.dynamic_update_slice_in_dim(key_grads, old_key + grad_key, key_first, 0)
            old_value = lax.dynamic_slice_in_dim(value_grads, key_first, block_rows, 0)
            value_grads = lax.dynamic_update_slice_in_dim(value_grads, old_value + grad_value, key_first, 0)
            return (query_grad + grad_query, key_grads, value_grads), None

        zero_query = jnp.zeros((block_rows, KVH, group_size, HD), jnp.float32)
        (query_grad, key_grads, value_grads), unused = lax.scan(key_step, (zero_query, key_grads, value_grads), block_ids)
        return (key_grads, value_grads), query_grad

    zero_keys = jnp.zeros((TOKENS, KVH, HD), jnp.float32)
    (key_grads, value_grads), query_grads = lax.scan(query_step, (zero_keys, zero_keys), block_ids)
    grad_queries = query_grads.astype(jnp.bfloat16).reshape(TOKENS, QH * HD)
    grad_keys = key_grads.astype(jnp.bfloat16).reshape(TOKENS, KVH * HD)
    grad_values = value_grads.astype(jnp.bfloat16).reshape(TOKENS, KVH * HD)
    return (grad_queries, grad_keys, grad_values)
```

```python
import functools

import jax
import jax.numpy as jnp
from jax import lax
from jax.experimental import pallas as pl
from jax.experimental.pallas import tpu as pltpu
from jax.sharding import PartitionSpec as P

HD = 128
ROW = 4
BACK = 3
FAR = 1e30
MESH = pl.DeviceIdType.MESH


class Parts:
    def __init__(self, copies, whole, out_sem):
        self.copies, self.whole, self.out_sem = copies, whole, out_sem

    def start(self):
        for copy in self.copies:
            copy.start()

    def wait_send(self):
        pltpu.make_async_copy(self.whole, self.whole, self.out_sem).wait()


def kernel(
    planes,
    group,
    docs_ref,
    q_ref,
    k_ref,
    v_ref,
    o_ref,
    do_ref,
    norm_ref,
    dq_ref,
    dk_ref,
    dv_ref,
    o_vm,
    do_vm,
    qd_buf,
    relay_buf,
    qt_buf,
    kv_buf,
    kt_buf,
    stat_send,
    stat_recv,
    doc_rows,
    key_marks,
    acc_kv,
    acc_q,
    grad_send,
    core_recv,
    y_recv,
    z_recv,
    dq_send,
    dkv_send,
    local_sem,
    q_sem,
    q_out_sem,
    relay_sem,
    kv_sem,
    kv_in_out_sem,
    kv_out_sem,
    stat_sem,
    core_sem,
    y_sem,
    z_sem,
    grad_out_sem,
    result_sem,
    result_out_sem,
):
    rows = q_ref.shape[0]
    wide = 2 * rows
    unit = 2 * wide
    scale = HD ** (-0.5)
    batches = ((0, 2), (2, group))
    me = lax.axis_index("head")
    ctx = lax.axis_index("ctx")
    side, core = lax.div(me, 2), lax.rem(me, 2)
    plane, place = lax.div(ctx, ROW), lax.rem(ctx, ROW)
    half_plane = 2 * plane + core
    first_core, second_core = core == 0, core == 1
    has_before, has_after = plane >= 1, plane + 1 < planes
    to_core = lax.div(place, 2)
    stays = to_core == core
    my_slot = 2 * lax.rem(place, 2) + core

    core_twin = (ctx, 2 * side + 1 - core)
    side_twin = (ctx, 2 * (1 - side) + core)
    after_same, after_other = (ctx + ROW, me), (ctx + ROW, core_twin[1])
    before_same, before_other = (ctx - ROW, me), (ctx - ROW, core_twin[1])

    def columns(first, count=HD):
        if isinstance(first, int):
            return pl.ds(first, count)
        return pl.ds(pl.multiple_of(first, HD), count)

    def piece_rows(slot):
        return pl.ds(pl.multiple_of(slot * rows, rows), rows)

    def remote(src, dst, out_sem, in_sem, device):
        return pltpu.make_async_remote_copy(
            src_ref=src,
            dst_ref=dst,
            send_sem=out_sem,
            recv_sem=in_sem,
            device_id=device,
            device_id_type=MESH,
        )

    def arrived(ref, sem):
        pltpu.make_async_copy(ref, ref, sem).wait()

    load_o = pltpu.make_async_copy(o_ref, o_vm, local_sem.at[0])
    load_do = pltpu.make_async_copy(do_ref, do_vm, local_sem.at[1])
    load_o.start()
    load_do.start()

    barrier = pltpu.get_barrier_semaphore()

    def greet(device):
        pl.semaphore_signal(barrier, inc=1, device_id=device, device_id_type=MESH)

    for step in range(1, 2 * ROW):
        other = lax.rem(2 * place + core + step, 2 * ROW)
        greet((ROW * plane + lax.div(other, 2), 2 * side + lax.rem(other, 2)))
    greet(side_twin)

    @pl.when(has_after)
    def _():
        greet(after_same)

        @pl.when(second_core)
        def _():
            greet(after_other)

    @pl.when(has_before)
    def _():
        greet(before_same)

        @pl.when(first_core)
        def _():
            greet(before_other)

    pl.semaphore_wait(
        barrier,
        2 * ROW
        + jnp.minimum(planes - 1 - plane, 1) * (1 + core)
        + jnp.minimum(plane, 1) * (2 - core),
    )

    def spread(pairs, out_sem, in_sem, steps=(2, 1, 3)):
        for src, dst in pairs(place):

            @pl.when(stays)
            def _():
                pltpu.make_async_copy(src, dst, in_sem).start()

            @pl.when(jnp.logical_not(stays))
            def _():
                remote(src, dst, out_sem, in_sem, core_twin).start()

        for step in steps:
            other = lax.rem(place + step, ROW)
            for src, dst in pairs(other):
                remote(
                    src, dst, out_sem, in_sem, (ROW * plane + other, 2 * side + to_core)
                ).start()

    for part, ref in ((0, k_ref), (1, v_ref)):
        spread(
            lambda which: [
                (ref.at[:, columns(which * HD)], kv_buf.at[0, 0, part, piece_rows(my_slot), :])
            ],
            kv_in_out_sem.at[0],
            kv_sem.at[0, 0, part],
        )

    after, across, between = (lax.rem(place + step, ROW) for step in (1, 2, 3))
    whole_group = group * HD
    to_between = []
    for index, (x, end) in enumerate(batches):
        to_between.append(
            remote(
                do_ref.at[:, columns(across * whole_group + x * HD, (end - x) * HD)],
                relay_buf.at[:, x * HD : end * HD],
                relay_sem.at[0, index],
                relay_sem.at[1, index],
                (ROW * plane + between, me),
            )
        )
    for index, (x, end) in enumerate(batches):
        to_between[index].start()
        for part, ref, steps in ((0, q_ref, (2, 1, 3)), (1, do_ref, (1, 3))):

            def head_pairs(which):
                cols = columns((which * group + x) * HD, (end - x) * HD)
                return [(ref.at[:, cols], qd_buf.at[part, piece_rows(my_slot), x * HD : end * HD])]

            spread(head_pairs, q_out_sem.at[part], q_sem.at[index], steps)

    load_o.wait()
    load_do.wait()

    def delta_step(which, carry):
        for x in range(group):
            cols = columns((which * group + x) * HD)
            products = do_vm[:, cols].astype(jnp.float32) * o_vm[:, cols].astype(jnp.float32)
            stat_send[which, pl.ds(8 + x, 1), :] = jnp.sum(products.T, axis=0, keepdims=True)
        return carry

    lax.fori_loop(0, ROW, delta_step, 0)
    for which in range(ROW):
        stat_send[which, 0:group, :] = norm_ref[which * group : (which + 1) * group, :]
    spread(
        lambda which: [(stat_send.at[which], stat_recv.at[my_slot])],
        stat_sem.at[0],
        stat_sem.at[1],
    )

    def pass_on(source, target, out, device):
        copies = [
            remote(
                kv_buf.at[source[0], source[1], part],
                kv_buf.at[target[0], target[1], part],
                kv_out_sem.at[out],
                kv_sem.at[target[0], target[1], part],
                device,
            )
            for part in range(2)
        ]
        return Parts(copies, kv_buf.at[0, 0], kv_out_sem.at[out])

    own_to_side = pass_on((0, 0), (0, 1), 0, side_twin)
    own_to_after = pass_on((0, 0), (2, 0), 1, after_same)
    own_to_core = pass_on((0, 0), (1, 0), 2, core_twin)
    side_to_core = pass_on((0, 1), (1, 1), 3, core_twin)
    before_to_side = pass_on((2, 0), (2, 1), 4, side_twin)
    to_second = (3 - 2 * core, 0)
    before_to_core = pass_on((2, 0), to_second, 5, core_twin)
    before_to_after = pass_on((2, 0), (3, 0), 6, after_other)
    to_second_side = (3 - 2 * core, 1)
    before_side_to_core = pass_on((2, 1), to_second_side, 7, core_twin)
    far_to_side = pass_on((3, 0), (3, 1), 8, side_twin)

    def has(k):
        return half_plane >= k

    def wait_kv(k, other, *sends):
        for part in range(2):
            arrived(kv_buf.at[k, other, part], kv_sem.at[k, other, part])
            for condition, send in sends:
                if condition is None:
                    send.copies[part].start()
                else:
                    pl.when(condition)(send.copies[part].start)
        kt_buf[k, other] = kv_buf[k, other, 0].T

    wait_kv(0, 0, (has_after, own_to_after), (None, own_to_side), (first_core, own_to_core))

    acc_kv[...] = jnp.zeros_like(acc_kv)
    acc_q[...] = jnp.zeros_like(acc_q)
    column = lax.broadcasted_iota(jnp.int32, (1, unit), 1)
    places = half_plane * (2 * unit) + side * wide + column + jnp.where(column >= wide, wide, 0)

    def hand_on(index):
        x, end = batches[index]
        arrived(relay_buf.at[:, x * HD : end * HD], relay_sem.at[1, index])
        remote(
            relay_buf.at[:, x * HD : end * HD],
            qd_buf.at[1, piece_rows(2 * lax.rem(after, 2) + core), x * HD : end * HD],
            relay_sem.at[2, index],
            q_sem.at[index],
            (ROW * plane + between, 2 * side + lax.div(after, 2)),
        ).start()

    docs = docs_ref.shape[0]
    lane = lax.broadcasted_iota(jnp.int32, (1, HD), 1)
    doc_rows[...] = jnp.zeros_like(doc_rows)

    def doc_step(index, state):
        first, firsts, ends = state
        end = first + docs_ref[index]
        inside = (places >= first) & (places < end)
        doc_rows[pl.ds(index, 1), :] = jnp.where(inside, 0.0, -FAR)
        here = lane == index
        return end, jnp.where(here, first, firsts), jnp.where(here, end, ends)

    nothing = jnp.zeros((1, HD), jnp.int32)
    unused, doc_firsts, doc_ends = lax.fori_loop(
        0, docs, doc_step, (jnp.int32(0), nothing, nothing)
    )
    hand_on(0)
    query_marks = doc_rows[...].astype(jnp.bfloat16)
    for k in range(BACK + 1):
        for other in range(2):
            row = lax.broadcasted_iota(jnp.int32, (unit, HD), 0)
            row = row + jnp.where(row >= wide, wide, 0)
            key_side = side + other * (1 - 2 * side)
            row = row + ((half_plane - k) * (2 * unit) + key_side * wide)
            lanes = lax.broadcasted_iota(jnp.int32, (unit, HD), 1)
            mark = ((row >= doc_firsts) & (row < doc_ends)) | ((lanes >= docs) & (lanes < docs + 3))
            key_marks[k, other] = jnp.where(mark, 1.0, 0.0).astype(jnp.bfloat16)

    arrived(stat_recv, stat_sem.at[1])

    def three_parts(value):
        high = value.astype(jnp.bfloat16).astype(jnp.float32)
        rest = value - high
        middle = rest.astype(jnp.bfloat16).astype(jnp.float32)
        row = lax.broadcasted_iota(jnp.int32, (HD, rows), 0)
        parts = jnp.where(row == docs, high, jnp.where(row == docs + 1, middle, rest - middle))
        return jnp.where((row >= docs) & (row < docs + 3), parts, 0.0).astype(jnp.bfloat16)

    for source in range(4):
        span = slice(source * rows, (source + 1) * rows)
        for x in range(group):
            norm = stat_recv[source, x : x + 1, :] * (-1.0 / scale)
            qt_buf[x, 0, HD : 2 * HD, span] = query_marks[:, span] + three_parts(norm)
            qt_buf[x, 1, HD : 2 * HD, span] = three_parts(-stat_recv[source, 8 + x : 9 + x, :])

    def dot(left, right):
        return jnp.dot(left, right, preferred_element_type=jnp.float32)

    def beside(left, right):
        return jnp.concatenate([left, right], axis=1)

    def weigh(k, other, x, i0, j0, jn, diagonal_from=None):
        seen = slice(i0, i0 + wide)
        held = slice(j0, j0 + jn)
        marks = key_marks[k, other, held, :]
        scores = dot(beside(kv_buf[k, other, 0, held, :], marks), qt_buf[x, 0, :, seen])
        weight_grads = dot(beside(kv_buf[k, other, 1, held, :], marks), qt_buf[x, 1, :, seen])
        weights = jnp.exp(scores * scale)
        if diagonal_from is not None:
            key_places = lax.broadcasted_iota(jnp.int32, (wide, wide), 0)
            query_places = lax.broadcasted_iota(jnp.int32, (wide, wide), 1)
            cut = diagonal_from - j0
            later = jnp.where(key_places <= query_places, weights[cut : cut + wide], 0.0)
            weights = jnp.concatenate([weights[0:cut], later], axis=0) if cut else later
        score_grads = weights * weight_grads
        return weights.astype(jnp.bfloat16), score_grads.astype(jnp.bfloat16)

    def rows_of(x, part, first, end):
        return qd_buf[part, first:end, columns(x * HD)]

    def whole_tile(k, other, x):
        weights_a, grads_a = weigh(k, other, x, 0, 0, unit)
        weights_b, grads_b = weigh(k, other, x, wide, 0, unit)
        grads = beside(grads_a, grads_b)
        value_part = dot(beside(weights_a, weights_b), rows_of(x, 1, 0, unit))
        key_part = dot(grads, rows_of(x, 0, 0, unit))
        query_part = dot(kt_buf[k, other], grads)
        acc_kv[k, other, 1] += value_part
        acc_kv[k, other, 0] += key_part
        acc_q[x] += query_part

    def lower_tile(k, other, x, diagonal):
        weights_a, grads_a = weigh(k, other, x, 0, 0, wide, 0 if diagonal else None)
        weights_b, grads_b = weigh(k, other, x, wide, 0, unit, wide if diagonal else None)
        for part, a, b in ((1, weights_a, weights_b), (0, grads_a, grads_b)):
            acc_kv[k, other, part, 0:wide, :] += dot(beside(a, b[0:wide]), rows_of(x, part, 0, unit))
            acc_kv[k, other, part, wide:unit, :] += dot(
                b[wide:unit], rows_of(x, part, wide, unit)
            )
        acc_q[x, :, 0:wide] += dot(kt_buf[k, other, :, 0:wide], grads_a)
        acc_q[x, :, wide:unit] += dot(kt_buf[k, other], grads_b)

    def upper_tile(k, other, x):
        weights_a, grads_a = weigh(k, other, x, 0, 0, unit)
        weights_b, grads_b = weigh(k, other, x, wide, wide, wide)
        for part, a, b in ((1, weights_a, weights_b), (0, grads_a, grads_b)):
            acc_kv[k, other, part, 0:wide, :] += dot(a[0:wide], rows_of(x, part, 0, wide))
            acc_kv[k, other, part, wide:unit, :] += dot(beside(a[wide:unit], b), rows_of(x, part, 0, unit))
        acc_q[x, :, 0:wide] += dot(kt_buf[k, other], grads_a)
        acc_q[x, :, wide:unit] += dot(kt_buf[k, other, :, wide:unit], grads_b)

    def corner_tile(k, other, x, i0, j0):
        weights, grads = weigh(k, other, x, i0, j0, wide)
        seen, held = slice(i0, i0 + wide), slice(j0, j0 + wide)
        acc_kv[k, other, 1, held, :] += dot(weights, rows_of(x, 1, i0, i0 + wide))
        acc_kv[k, other, 0, held, :] += dot(grads, rows_of(x, 0, i0, i0 + wide))
        acc_q[x, :, seen] += dot(kt_buf[k, other, :, held], grads)

    def give(k, other, slots, slot, sems, device):
        out_sem = grad_out_sem.at[k, other]
        copies = [
            remote(
                grad_send.at[k, other, part],
                slots.at[slot, part],
                out_sem,
                sems.at[slot, part],
                device,
            )
            for part in range(2)
        ]
        return Parts(copies, grad_send.at[k, other], out_sem)

    def round_grads(k, other):
        grad_send[k, other] = acc_kv[k, other].astype(jnp.bfloat16)

    def take(k, other, slots, slot, sems, parts=(0, 1)):
        for part in parts:
            arrived(slots.at[slot, part], sems.at[slot, part])
            acc_kv[k, other, part] += slots[slot, part].astype(jnp.float32)

    far_side_given = give(3, 1, y_recv, 2, y_sem, side_twin)
    far_side_given_core = give(3, 1, core_recv, 3, core_sem, core_twin)
    far_given = give(3, 0, z_recv, 1, z_sem, before_other)
    far_given_core = give(3, 0, core_recv, 2, core_sem, core_twin)
    near_given = give(1, 0, core_recv, 0, core_sem, core_twin)
    near_side_given = give(1, 1, core_recv, 1, core_sem, core_twin)
    middle_given = give(2, 0, z_recv, 0, z_sem, before_same)
    middle_side_given = give(2, 1, y_recv, 1, y_sem, side_twin)
    own_side_given = give(0, 1, y_recv, 0, y_sem, side_twin)

    def gather_back(src, dst, out_sem, in_sem):
        for slot in range(4):
            part = src.at[slot * rows : (slot + 1) * rows, :]
            owner = 2 * core + slot // 2

            @pl.when((place == owner) & (core == slot % 2))
            def _():
                pltpu.make_async_copy(part, dst, in_sem).start()

            @pl.when((place != owner) | (core != slot % 2))
            def _():
                remote(
                    part, dst, out_sem, in_sem, (ROW * plane + owner, 2 * side + slot % 2)
                ).start()

    early = batches[0][1]

    def far_side_tile(x):
        @pl.when(side == 0)
        def _():
            upper_tile(3, 1, x)

        @pl.when(side == 1)
        def _():
            corner_tile(3, 1, x, 0, wide)

    def near_side_tile(x):
        @pl.when(side == 0)
        def _():
            corner_tile(0, 1, x, wide, 0)

        @pl.when(side == 1)
        def _():
            lower_tile(0, 1, x, False)

    def finish_query(x):
        dq_send[:, columns(x * HD)] = (acc_q[x].T * scale).astype(jnp.bfloat16)

    def return_query(first, count):
        gather_back(
            dq_send.at[:, columns(first * HD, count * HD)],
            dq_ref.at[:, columns((place * group + first) * HD, count * HD)],
            result_out_sem.at[0],
            result_sem.at[0],
        )

    def wait_q(index):
        first, end = batches[index]
        arrived(qd_buf.at[:, :, first * HD : end * HD], q_sem.at[index])
        for x in range(first, end):
            for part in range(2):
                qt_buf[x, part, 0:HD, :] = qd_buf[part, :, x * HD : (x + 1) * HD].T

    def over_heads(tile, first=early, end=group):
        def step(x, carry):
            tile(x)
            return carry

        lax.fori_loop(first, end, step, 0)

    def early_heads(tile):
        over_heads(tile, 0, early)

    @pl.when(has_before)
    def _():
        wait_kv(
            2,
            0,
            (second_core & has_after, before_to_after),
            (None, before_to_side),
            (None, before_to_core),
        )

    wait_q(0)
    early_heads(lambda x: lower_tile(0, 0, x, True))
    hand_on(1)

    @pl.when(has(1))
    def _():
        wait_kv(1, 0)

    def early_same_unit(index, carry):
        k = 2 - index

        @pl.when(has(k))
        def _():
            early_heads(lambda x: whole_tile(k, 0, x))

        return carry

    lax.fori_loop(0, 2, early_same_unit, 0)
    wait_kv(0, 1, (first_core, side_to_core))

    @pl.when(has(3))
    def _():
        wait_kv(3, 0, (first_core, far_to_side))
        early_heads(lambda x: upper_tile(3, 0, x))

    early_heads(near_side_tile)

    @pl.when(has_before)
    def _():
        wait_kv(2, 1, (None, before_side_to_core))

    @pl.when(has(1))
    def _():
        wait_kv(1, 1)

    def early_other_unit(index, carry):
        k = 2 - index

        @pl.when(has(k))
        def _():
            early_heads(lambda x: whole_tile(k, 1, x))

        return carry

    lax.fori_loop(0, 2, early_other_unit, 0)

    @pl.when(has(3))
    def _():
        wait_kv(3, 1)
        early_heads(far_side_tile)

    for x in range(early):
        finish_query(x)
    return_query(0, early)
    wait_q(1)

    @pl.when(has(3))
    def _():
        over_heads(far_side_tile)
        round_grads(3, 1)
        pl.when(first_core)(far_side_given.start)
        pl.when(second_core)(far_side_given_core.start)

    def other_unit(index, carry):
        k = 1 + index

        @pl.when(has(k))
        def _():
            over_heads(lambda x: whole_tile(k, 1, x))

        @pl.when((index == 0) & has(1))
        def _():
            round_grads(1, 1)
            near_side_given.start()

        return carry

    lax.fori_loop(0, 2, other_unit, 0)

    @pl.when(has_before)
    def _():
        take(2, 1, core_recv, 3 - 2 * core, core_sem)
        round_grads(2, 1)
        middle_side_given.start()

    @pl.when(has(3))
    def _():
        over_heads(lambda x: upper_tile(3, 0, x))

        @pl.when(first_core)
        def _():
            take(3, 0, y_recv, 2, y_sem)

        round_grads(3, 0)
        pl.when(first_core)(far_given.start)
        pl.when(second_core)(far_given_core.start)

    over_heads(near_side_tile)

    @pl.when(first_core)
    def _():
        take(0, 1, core_recv, 1, core_sem)

    round_grads(0, 1)
    own_side_given.start()

    def same_unit(index, carry):
        k = 1 + index

        @pl.when(has(k))
        def _():
            over_heads(lambda x: whole_tile(k, 0, x))

        @pl.when((index == 0) & has(1))
        def _():
            round_grads(1, 0)
            near_given.start()

        return carry

    lax.fori_loop(0, 2, same_unit, 0)

    @pl.when(has_before)
    def _():
        take(2, 0, core_recv, 2 - 2 * core, core_sem)
        take(2, 0, y_recv, 1, y_sem)

        @pl.when(second_core & has_after)
        def _():
            take(2, 0, z_recv, 1, z_sem)

        round_grads(2, 0)
        middle_given.start()

    def own_head(x):
        lower_tile(0, 0, x, True)
        finish_query(x)
        return_query(x, 1)

    over_heads(own_head)

    for part, ref, factor in ((0, dk_ref, scale), (1, dv_ref, 1.0)):

        @pl.when(first_core)
        def _():
            take(0, 0, core_recv, 0, core_sem, (part,))

        take(0, 0, y_recv, 0, y_sem, (part,))

        @pl.when(has_after)
        def _():
            take(0, 0, z_recv, 0, z_sem, (part,))

        dkv_send[part] = (acc_kv[0, 0, part] * factor).astype(jnp.bfloat16)
        gather_back(
            dkv_send.at[part],
            ref.at[:, columns(place * HD)],
            result_out_sem.at[1 + part],
            result_sem.at[1 + part],
        )

    def drain(away):
        arrived(kv_buf.at[0, 0, :, 0:away, :], kv_in_out_sem.at[0])
        arrived(qd_buf.at[0, 0:away, :], q_out_sem.at[0])
        arrived(qd_buf.at[1, 0 : away - rows, :], q_out_sem.at[1])
        arrived(stat_recv.at[0 : away // rows], stat_sem.at[0])

    @pl.when(stays)
    def _():
        drain(unit - rows)

    @pl.when(jnp.logical_not(stays))
    def _():
        drain(unit)

    for index, (x, end) in enumerate(batches):
        arrived(relay_buf.at[:, x * HD : end * HD], relay_sem.at[2, index])
        to_between[index].wait_send()
    own_to_side.wait_send()
    own_side_given.wait_send()

    @pl.when(has_after)
    def _():
        own_to_after.wait_send()

    @pl.when(first_core)
    def _():
        own_to_core.wait_send()
        side_to_core.wait_send()

    @pl.when(has_before)
    def _():
        before_to_side.wait_send()
        before_to_core.wait_send()
        before_side_to_core.wait_send()
        middle_given.wait_send()
        middle_side_given.wait_send()

    @pl.when(second_core & has_before & has_after)
    def _():
        before_to_after.wait_send()

    @pl.when(has(1))
    def _():
        near_given.wait_send()
        near_side_given.wait_send()

    @pl.when(has(3))
    def _():
        far_given.wait_send()
        far_side_given.wait_send()

        @pl.when(first_core)
        def _():
            far_to_side.wait_send()

    def drain_back(away):
        arrived(dq_send.at[0:away, :], result_out_sem.at[0])
        for part in range(2):
            arrived(dkv_send.at[part, 0:away, :], result_out_sem.at[1 + part])

    @pl.when(stays)
    def _():
        drain_back(unit - rows)

    @pl.when(jnp.logical_not(stays))
    def _():
        drain_back(unit)

    for index, ref in enumerate((dq_ref, dk_ref, dv_ref)):
        arrived(ref, result_sem.at[index])


def hand_over(dq_in, dk_in, dv_in, dq_out, dk_out, dv_out, dq_vm, dk_vm, dv_vm, sems):
    ways = ((dk_in, dk_vm, dk_out), (dv_in, dv_vm, dv_out), (dq_in, dq_vm, dq_out))
    ins = [pltpu.make_async_copy(src, vm, sems.at[0, i]) for i, (src, vm, dst) in enumerate(ways)]
    outs = [pltpu.make_async_copy(vm, dst, sems.at[1, i]) for i, (src, vm, dst) in enumerate(ways)]
    for copy in ins:
        copy.start()
    for first, second in zip(ins, outs):
        first.wait()
        second.start()
    for copy in outs:
        copy.wait()


def body(queries, keys, values, attn_out, grad_out, log_norm, doc_lengths):
    heads = lax.axis_size("head")
    planes = lax.axis_size("ctx") // ROW
    rows = queries.shape[0]
    unit = rows * heads
    group = queries.shape[1] // keys.shape[1]
    low, full = jnp.bfloat16, jnp.float32
    anywhere = pl.BlockSpec(memory_space=pl.ANY)
    pairs = unit * unit * 6.5 * group
    dma = pltpu.SemaphoreType.DMA
    results = (
        jax.ShapeDtypeStruct(queries.shape, low),
        jax.ShapeDtypeStruct(keys.shape, low),
        jax.ShapeDtypeStruct(values.shape, low),
    )
    gradients = pl.pallas_call(
        functools.partial(kernel, planes, group),
        out_shape=results,
        in_specs=[pl.BlockSpec(memory_space=pltpu.SMEM)]
        + [anywhere] * 5
        + [pl.BlockSpec(memory_space=pltpu.VMEM)],
        out_specs=(anywhere, anywhere, anywhere),
        scratch_shapes=[
            pltpu.VMEM(attn_out.shape, low),
            pltpu.VMEM(grad_out.shape, low),
            pltpu.VMEM((2, unit, group * HD), low),
            pltpu.VMEM((rows, group * HD), low),
            pltpu.VMEM((group, 2, 2 * HD, unit), low),
            pltpu.VMEM((BACK + 1, 2, 2, unit, HD), low),
            pltpu.VMEM((BACK + 1, 2, HD, unit), low),
            pltpu.VMEM((ROW, 16, rows), full),
            pltpu.VMEM((4, 16, rows), full),
            pltpu.VMEM((HD, unit), full),
            pltpu.VMEM((BACK + 1, 2, unit, HD), low),
            pltpu.VMEM((BACK + 1, 2, 2, unit, HD), full),
            pltpu.VMEM((group, HD, unit), full),
            pltpu.VMEM((BACK + 1, 2, 2, unit, HD), low),
            pltpu.VMEM((4, 2, unit, HD), low),
            pltpu.VMEM((3, 2, unit, HD), low),
            pltpu.VMEM((2, 2, unit, HD), low),
            pltpu.VMEM((unit, group * HD), low),
            pltpu.VMEM((2, unit, HD), low),
            dma((2,)),
            dma((2,)),
            dma((2,)),
            dma((3, 2)),
            dma((BACK + 1, 2, 2)),
            dma((1,)),
            dma((9,)),
            dma((2,)),
            dma((4, 2)),
            dma((3, 2)),
            dma((2, 2)),
            dma((BACK + 1, 2)),
            dma((3,)),
            dma((3,)),
        ],
        compiler_params=pltpu.CompilerParams(
            collective_id=0, has_side_effects=True, vmem_limit_bytes=63 * 1024 * 1024
        ),
        cost_estimate=pl.CostEstimate(
            flops=int(10 * pairs * HD), bytes_accessed=8 * 1024 * 1024, transcendentals=int(pairs)
        ),
    )(doc_lengths, queries, keys, values, attn_out, grad_out, log_norm)
    return pl.pallas_call(
        hand_over,
        out_shape=results,
        in_specs=[anywhere] * 3,
        out_specs=(anywhere,) * 3,
        scratch_shapes=[pltpu.VMEM(result.shape, low) for result in results] + [dma((2, 3))],
        compiler_params=pltpu.CompilerParams(vmem_limit_bytes=63 * 1024 * 1024),
        cost_estimate=pl.CostEstimate(flops=0, bytes_accessed=2 * 1024 * 1024, transcendentals=0),
    )(*gradients)


def solution(mesh):
    spread = P(("ctx", "head"), None)
    return jax.shard_map(
        body,
        mesh=mesh,
        in_specs=(spread, spread, spread, spread, spread, P(None, ("ctx", "head")), P()),
        out_specs=(spread, spread, spread),
        check_vma=False,
    )
```

```python
import functools

import jax
import jax.numpy as jnp
from jax import lax
from jax.experimental import pallas as pl
from jax.experimental.pallas import tpu as pltpu
from jax.sharding import PartitionSpec as P

HD = 128
ROW = 4
BACK = 3
FAR = 1e30
MESH = pl.DeviceIdType.MESH


class Parts:
    def __init__(self, copies, whole, out_sem):
        self.copies, self.whole, self.out_sem = copies, whole, out_sem

    def start(self):
        for copy in self.copies:
            copy.start()

    def wait_send(self):
        pltpu.make_async_copy(self.whole, self.whole, self.out_sem).wait()


def kernel(
    planes,
    group,
    docs_ref,
    q_ref,
    k_ref,
    v_ref,
    o_ref,
    do_ref,
    norm_ref,
    dq_ref,
    dk_ref,
    dv_ref,
    o_vm,
    do_vm,
    qd_buf,
    relay_buf,
    qt_buf,
    kv_buf,
    kt_buf,
    stat_send,
    stat_recv,
    doc_rows,
    key_marks,
    acc_kv,
    acc_q,
    grad_send,
    core_recv,
    y_recv,
    z_recv,
    dq_send,
    dkv_send,
    local_sem,
    q_sem,
    q_out_sem,
    relay_sem,
    kv_sem,
    kv_in_out_sem,
    kv_out_sem,
    stat_sem,
    core_sem,
    y_sem,
    z_sem,
    grad_out_sem,
    result_sem,
    result_out_sem,
):
    rows = q_ref.shape[0]
    wide = 2 * rows
    unit = 2 * wide
    scale = HD ** (-0.5)
    batches = ((0, 2), (2, group))
    me = lax.axis_index("head")
    ctx = lax.axis_index("ctx")
    side, core = lax.div(me, 2), lax.rem(me, 2)
    plane, place = lax.div(ctx, ROW), lax.rem(ctx, ROW)
    half_plane = 2 * plane + core
    first_core, second_core = core == 0, core == 1
    has_before, has_after = plane >= 1, plane + 1 < planes
    to_core = lax.div(place, 2)
    stays = to_core == core
    my_slot = 2 * lax.rem(place, 2) + core

    core_twin = (ctx, 2 * side + 1 - core)
    side_twin = (ctx, 2 * (1 - side) + core)
    after_same, after_other = (ctx + ROW, me), (ctx + ROW, core_twin[1])
    before_same, before_other = (ctx - ROW, me), (ctx - ROW, core_twin[1])

    def columns(first, count=HD):
        if isinstance(first, int):
            return pl.ds(first, count)
        return pl.ds(pl.multiple_of(first, HD), count)

    def piece_rows(slot):
        return pl.ds(pl.multiple_of(slot * rows, rows), rows)

    def remote(src, dst, out_sem, in_sem, device):
        return pltpu.make_async_remote_copy(
            src_ref=src,
            dst_ref=dst,
            send_sem=out_sem,
            recv_sem=in_sem,
            device_id=device,
            device_id_type=MESH,
        )

    def arrived(ref, sem):
        pltpu.make_async_copy(ref, ref, sem).wait()

    load_o = pltpu.make_async_copy(o_ref, o_vm, local_sem.at[0])
    load_do = pltpu.make_async_copy(do_ref, do_vm, local_sem.at[1])
    load_o.start()
    load_do.start()

    barrier = pltpu.get_barrier_semaphore()

    def greet(device):
        pl.semaphore_signal(barrier, inc=1, device_id=device, device_id_type=MESH)

    for step in range(1, 2 * ROW):
        other = lax.rem(2 * place + core + step, 2 * ROW)
        greet((ROW * plane + lax.div(other, 2), 2 * side + lax.rem(other, 2)))
    greet(side_twin)

    @pl.when(has_after)
    def _():
        greet(after_same)

        @pl.when(second_core)
        def _():
            greet(after_other)

    @pl.when(has_before)
    def _():
        greet(before_same)

        @pl.when(first_core)
        def _():
            greet(before_other)

    pl.semaphore_wait(
        barrier,
        2 * ROW
        + jnp.minimum(planes - 1 - plane, 1) * (1 + core)
        + jnp.minimum(plane, 1) * (2 - core),
    )

    def spread(pairs, out_sem, in_sem, steps=(2, 1, 3)):
        for src, dst in pairs(place):

            @pl.when(stays)
            def _():
                pltpu.make_async_copy(src, dst, in_sem).start()

            @pl.when(jnp.logical_not(stays))
            def _():
                remote(src, dst, out_sem, in_sem, core_twin).start()

        for step in steps:
            other = lax.rem(place + step, ROW)
            for src, dst in pairs(other):
                remote(
                    src, dst, out_sem, in_sem, (ROW * plane + other, 2 * side + to_core)
                ).start()

    for part, ref in ((0, k_ref), (1, v_ref)):
        spread(
            lambda which: [
                (ref.at[:, columns(which * HD)], kv_buf.at[0, 0, part, piece_rows(my_slot), :])
            ],
            kv_in_out_sem.at[0],
            kv_sem.at[0, 0, part],
        )

    after, across, between = (lax.rem(place + step, ROW) for step in (1, 2, 3))
    whole_group = group * HD
    to_between = []
    for index, (x, end) in enumerate(batches):
        to_between.append(
            remote(
                do_ref.at[:, columns(across * whole_group + x * HD, (end - x) * HD)],
                relay_buf.at[:, x * HD : end * HD],
                relay_sem.at[0, index],
                relay_sem.at[1, index],
                (ROW * plane + between, me),
            )
        )
    for index, (x, end) in enumerate(batches):
        to_between[index].start()
        for part, ref, steps in ((0, q_ref, (2, 1, 3)), (1, do_ref, (1, 3))):

            def head_pairs(which):
                cols = columns((which * group + x) * HD, (end - x) * HD)
                return [(ref.at[:, cols], qd_buf.at[part, piece_rows(my_slot), x * HD : end * HD])]

            spread(head_pairs, q_out_sem.at[part], q_sem.at[index], steps)

    load_o.wait()
    load_do.wait()

    def delta_step(which, carry):
        for x in range(group):
            cols = columns((which * group + x) * HD)
            products = do_vm[:, cols].astype(jnp.float32) * o_vm[:, cols].astype(jnp.float32)
            stat_send[which, pl.ds(8 + x, 1), :] = jnp.sum(products.T, axis=0, keepdims=True)
        return carry

    lax.fori_loop(0, ROW, delta_step, 0)
    for which in range(ROW):
        stat_send[which, 0:group, :] = norm_ref[which * group : (which + 1) * group, :]
    spread(
        lambda which: [(stat_send.at[which], stat_recv.at[my_slot])],
        stat_sem.at[0],
        stat_sem.at[1],
    )

    def pass_on(source, target, out, device):
        copies = [
            remote(
                kv_buf.at[source[0], source[1], part],
                kv_buf.at[target[0], target[1], part],
                kv_out_sem.at[out],
                kv_sem.at[target[0], target[1], part],
                device,
            )
            for part in range(2)
        ]
        return Parts(copies, kv_buf.at[0, 0], kv_out_sem.at[out])

    own_to_side = pass_on((0, 0), (0, 1), 0, side_twin)
    own_to_after = pass_on((0, 0), (2, 0), 1, after_same)
    own_to_core = pass_on((0, 0), (1, 0), 2, core_twin)
    side_to_core = pass_on((0, 1), (1, 1), 3, core_twin)
    before_to_side = pass_on((2, 0), (2, 1), 4, side_twin)
    to_second = (3 - 2 * core, 0)
    before_to_core = pass_on((2, 0), to_second, 5, core_twin)
    before_to_after = pass_on((2, 0), (3, 0), 6, after_other)
    to_second_side = (3 - 2 * core, 1)
    before_side_to_core = pass_on((2, 1), to_second_side, 7, core_twin)
    far_to_side = pass_on((3, 0), (3, 1), 8, side_twin)

    def has(k):
        return half_plane >= k

    def wait_kv(k, other, *sends):
        for part in range(2):
            arrived(kv_buf.at[k, other, part], kv_sem.at[k, other, part])
            for condition, send in sends:
                if condition is None:
                    send.copies[part].start()
                else:
                    pl.when(condition)(send.copies[part].start)
        kt_buf[k, other] = kv_buf[k, other, 0].T

    wait_kv(0, 0, (has_after, own_to_after), (None, own_to_side), (first_core, own_to_core))

    acc_kv[...] = jnp.zeros_like(acc_kv)
    acc_q[...] = jnp.zeros_like(acc_q)
    column = lax.broadcasted_iota(jnp.int32, (1, unit), 1)
    places = half_plane * (2 * unit) + side * wide + column + jnp.where(column >= wide, wide, 0)

    def hand_on(index):
        x, end = batches[index]
        arrived(relay_buf.at[:, x * HD : end * HD], relay_sem.at[1, index])
        remote(
            relay_buf.at[:, x * HD : end * HD],
            qd_buf.at[1, piece_rows(2 * lax.rem(after, 2) + core), x * HD : end * HD],
            relay_sem.at[2, index],
            q_sem.at[index],
            (ROW * plane + between, 2 * side + lax.div(after, 2)),
        ).start()

    docs = docs_ref.shape[0]
    lane = lax.broadcasted_iota(jnp.int32, (1, HD), 1)
    doc_rows[...] = jnp.zeros_like(doc_rows)

    def doc_step(index, state):
        first, firsts, ends = state
        end = first + docs_ref[index]
        inside = (places >= first) & (places < end)
        doc_rows[pl.ds(index, 1), :] = jnp.where(inside, 0.0, -FAR)
        here = lane == index
        return end, jnp.where(here, first, firsts), jnp.where(here, end, ends)

    nothing = jnp.zeros((1, HD), jnp.int32)
    unused, doc_firsts, doc_ends = lax.fori_loop(
        0, docs, doc_step, (jnp.int32(0), nothing, nothing)
    )
    hand_on(0)
    query_marks = doc_rows[...].astype(jnp.bfloat16)
    for k in range(BACK + 1):
        for other in range(2):
            row = lax.broadcasted_iota(jnp.int32, (unit, HD), 0)
            row = row + jnp.where(row >= wide, wide, 0)
            key_side = side + other * (1 - 2 * side)
            row = row + ((half_plane - k) * (2 * unit) + key_side * wide)
            lanes = lax.broadcasted_iota(jnp.int32, (unit, HD), 1)
            mark = ((row >= doc_firsts) & (row < doc_ends)) | ((lanes >= docs) & (lanes < docs + 3))
            key_marks[k, other] = jnp.where(mark, 1.0, 0.0).astype(jnp.bfloat16)

    arrived(stat_recv, stat_sem.at[1])

    def three_parts(value):
        high = value.astype(jnp.bfloat16).astype(jnp.float32)
        rest = value - high
        middle = rest.astype(jnp.bfloat16).astype(jnp.float32)
        row = lax.broadcasted_iota(jnp.int32, (HD, rows), 0)
        parts = jnp.where(row == docs, high, jnp.where(row == docs + 1, middle, rest - middle))
        return jnp.where((row >= docs) & (row < docs + 3), parts, 0.0).astype(jnp.bfloat16)

    for source in range(4):
        span = slice(source * rows, (source + 1) * rows)
        for x in range(group):
            norm = stat_recv[source, x : x + 1, :] * (-1.0 / scale)
            qt_buf[x, 0, HD : 2 * HD, span] = query_marks[:, span] + three_parts(norm)
            qt_buf[x, 1, HD : 2 * HD, span] = three_parts(-stat_recv[source, 8 + x : 9 + x, :])

    def dot(left, right):
        return jnp.dot(left, right, preferred_element_type=jnp.float32)

    def beside(left, right):
        return jnp.concatenate([left, right], axis=1)

    def weigh(k, other, x, i0, j0, jn, diagonal_from=None):
        seen = slice(i0, i0 + wide)
        held = slice(j0, j0 + jn)
        marks = key_marks[k, other, held, :]
        scores = dot(beside(kv_buf[k, other, 0, held, :], marks), qt_buf[x, 0, :, seen])
        weight_grads = dot(beside(kv_buf[k, other, 1, held, :], marks), qt_buf[x, 1, :, seen])
        weights = jnp.exp(scores * scale)
        if diagonal_from is not None:
            key_places = lax.broadcasted_iota(jnp.int32, (wide, wide), 0)
            query_places = lax.broadcasted_iota(jnp.int32, (wide, wide), 1)
            cut = diagonal_from - j0
            later = jnp.where(key_places <= query_places, weights[cut : cut + wide], 0.0)
            weights = jnp.concatenate([weights[0:cut], later], axis=0) if cut else later
        score_grads = weights * weight_grads
        return weights.astype(jnp.bfloat16), score_grads.astype(jnp.bfloat16)

    def rows_of(x, part, first, end):
        return qd_buf[part, first:end, columns(x * HD)]

    def whole_tile(k, other, x):
        weights_a, grads_a = weigh(k, other, x, 0, 0, unit)
        weights_b, grads_b = weigh(k, other, x, wide, 0, unit)
        grads = beside(grads_a, grads_b)
        value_part = dot(beside(weights_a, weights_b), rows_of(x, 1, 0, unit))
        key_part = dot(grads, rows_of(x, 0, 0, unit))
        query_part = dot(kt_buf[k, other], grads)
        acc_kv[k, other, 1] += value_part
        acc_kv[k, other, 0] += key_part
        acc_q[x] += query_part

    def lower_tile(k, other, x, diagonal):
        weights_a, grads_a = weigh(k, other, x, 0, 0, wide, 0 if diagonal else None)
        weights_b, grads_b = weigh(k, other, x, wide, 0, unit, wide if diagonal else None)
        for part, a, b in ((1, weights_a, weights_b), (0, grads_a, grads_b)):
            acc_kv[k, other, part, 0:wide, :] += dot(beside(a, b[0:wide]), rows_of(x, part, 0, unit))
            acc_kv[k, other, part, wide:unit, :] += dot(
                b[wide:unit], rows_of(x, part, wide, unit)
            )
        acc_q[x, :, 0:wide] += dot(kt_buf[k, other, :, 0:wide], grads_a)
        acc_q[x, :, wide:unit] += dot(kt_buf[k, other], grads_b)

    def upper_tile(k, other, x):
        weights_a, grads_a = weigh(k, other, x, 0, 0, unit)
        weights_b, grads_b = weigh(k, other, x, wide, wide, wide)
        for part, a, b in ((1, weights_a, weights_b), (0, grads_a, grads_b)):
            acc_kv[k, other, part, 0:wide, :] += dot(a[0:wide], rows_of(x, part, 0, wide))
            acc_kv[k, other, part, wide:unit, :] += dot(beside(a[wide:unit], b), rows_of(x, part, 0, unit))
        acc_q[x, :, 0:wide] += dot(kt_buf[k, other], grads_a)
        acc_q[x, :, wide:unit] += dot(kt_buf[k, other, :, wide:unit], grads_b)

    def corner_tile(k, other, x, i0, j0):
        weights, grads = weigh(k, other, x, i0, j0, wide)
        seen, held = slice(i0, i0 + wide), slice(j0, j0 + wide)
        acc_kv[k, other, 1, held, :] += dot(weights, rows_of(x, 1, i0, i0 + wide))
        acc_kv[k, other, 0, held, :] += dot(grads, rows_of(x, 0, i0, i0 + wide))
        acc_q[x, :, seen] += dot(kt_buf[k, other, :, held], grads)

    def give(k, other, slots, slot, sems, device):
        out_sem = grad_out_sem.at[k, other]
        copies = [
            remote(
                grad_send.at[k, other, part],
                slots.at[slot, part],
                out_sem,
                sems.at[slot, part],
                device,
            )
            for part in range(2)
        ]
        return Parts(copies, grad_send.at[k, other], out_sem)

    def round_grads(k, other):
        grad_send[k, other] = acc_kv[k, other].astype(jnp.bfloat16)

    def take(k, other, slots, slot, sems, parts=(0, 1)):
        for part in parts:
            arrived(slots.at[slot, part], sems.at[slot, part])
            acc_kv[k, other, part] += slots[slot, part].astype(jnp.float32)

    far_side_given = give(3, 1, y_recv, 2, y_sem, side_twin)
    far_side_given_core = give(3, 1, core_recv, 3, core_sem, core_twin)
    far_given = give(3, 0, z_recv, 1, z_sem, before_other)
    far_given_core = give(3, 0, core_recv, 2, core_sem, core_twin)
    near_given = give(1, 0, core_recv, 0, core_sem, core_twin)
    near_side_given = give(1, 1, core_recv, 1, core_sem, core_twin)
    middle_given = give(2, 0, z_recv, 0, z_sem, before_same)
    middle_side_given = give(2, 1, y_recv, 1, y_sem, side_twin)
    own_side_given = give(0, 1, y_recv, 0, y_sem, side_twin)

    def gather_back(src, dst, out_sem, in_sem):
        for slot in range(4):
            part = src.at[slot * rows : (slot + 1) * rows, :]
            owner = 2 * core + slot // 2

            @pl.when((place == owner) & (core == slot % 2))
            def _():
                pltpu.make_async_copy(part, dst, in_sem).start()

            @pl.when((place != owner) | (core != slot % 2))
            def _():
                remote(
                    part, dst, out_sem, in_sem, (ROW * plane + owner, 2 * side + slot % 2)
                ).start()

    early = batches[0][1]

    def far_side_tile(x):
        @pl.when(side == 0)
        def _():
            upper_tile(3, 1, x)

        @pl.when(side == 1)
        def _():
            corner_tile(3, 1, x, 0, wide)

    def near_side_tile(x):
        @pl.when(side == 0)
        def _():
            corner_tile(0, 1, x, wide, 0)

        @pl.when(side == 1)
        def _():
            lower_tile(0, 1, x, False)

    def finish_query(x):
        dq_send[:, columns(x * HD)] = (acc_q[x].T * scale).astype(jnp.bfloat16)

    def return_query(first, count):
        gather_back(
            dq_send.at[:, columns(first * HD, count * HD)],
            dq_ref.at[:, columns((place * group + first) * HD, count * HD)],
            result_out_sem.at[0],
            result_sem.at[0],
        )

    def wait_q(index):
        first, end = batches[index]
        arrived(qd_buf.at[:, :, first * HD : end * HD], q_sem.at[index])
        for x in range(first, end):
            for part in range(2):
                qt_buf[x, part, 0:HD, :] = qd_buf[part, :, x * HD : (x + 1) * HD].T

    def over_heads(tile, first=early, end=group):
        for x in range(first, end):
            tile(x)

    def early_heads(tile):
        over_heads(tile, 0, early)

    @pl.when(has_before)
    def _():
        wait_kv(
            2,
            0,
            (second_core & has_after, before_to_after),
            (None, before_to_side),
            (None, before_to_core),
        )

    wait_q(0)
    early_heads(lambda x: lower_tile(0, 0, x, True))
    hand_on(1)

    @pl.when(has(1))
    def _():
        wait_kv(1, 0)

    def early_same_unit(index, carry):
        k = 2 - index

        @pl.when(has(k))
        def _():
            early_heads(lambda x: whole_tile(k, 0, x))

        return carry

    lax.fori_loop(0, 2, early_same_unit, 0)
    wait_kv(0, 1, (first_core, side_to_core))

    @pl.when(has(3))
    def _():
        wait_kv(3, 0, (first_core, far_to_side))
        early_heads(lambda x: upper_tile(3, 0, x))

    early_heads(near_side_tile)

    @pl.when(has_before)
    def _():
        wait_kv(2, 1, (None, before_side_to_core))

    @pl.when(has(1))
    def _():
        wait_kv(1, 1)

    def early_other_unit(index, carry):
        k = 2 - index

        @pl.when(has(k))
        def _():
            early_heads(lambda x: whole_tile(k, 1, x))

        return carry

    lax.fori_loop(0, 2, early_other_unit, 0)

    @pl.when(has(3))
    def _():
        wait_kv(3, 1)
        early_heads(far_side_tile)

    for x in range(early):
        finish_query(x)
    return_query(0, early)
    wait_q(1)

    @pl.when(has(3))
    def _():
        over_heads(far_side_tile)
        round_grads(3, 1)
        pl.when(first_core)(far_side_given.start)
        pl.when(second_core)(far_side_given_core.start)

    def other_unit(index, carry):
        k = 1 + index

        @pl.when(has(k))
        def _():
            over_heads(lambda x: whole_tile(k, 1, x))

        @pl.when((index == 0) & has(1))
        def _():
            round_grads(1, 1)
            near_side_given.start()

        return carry

    lax.fori_loop(0, 2, other_unit, 0)

    @pl.when(has_before)
    def _():
        take(2, 1, core_recv, 3 - 2 * core, core_sem)
        round_grads(2, 1)
        middle_side_given.start()

    @pl.when(has(3))
    def _():
        over_heads(lambda x: upper_tile(3, 0, x))

        @pl.when(first_core)
        def _():
            take(3, 0, y_recv, 2, y_sem)

        round_grads(3, 0)
        pl.when(first_core)(far_given.start)
        pl.when(second_core)(far_given_core.start)

    over_heads(near_side_tile)

    @pl.when(first_core)
    def _():
        take(0, 1, core_recv, 1, core_sem)

    round_grads(0, 1)
    own_side_given.start()

    def same_unit(index, carry):
        k = 1 + index

        @pl.when(has(k))
        def _():
            over_heads(lambda x: whole_tile(k, 0, x))

        @pl.when((index == 0) & has(1))
        def _():
            round_grads(1, 0)
            near_given.start()

        return carry

    lax.fori_loop(0, 2, same_unit, 0)

    @pl.when(has_before)
    def _():
        take(2, 0, core_recv, 2 - 2 * core, core_sem)
        take(2, 0, y_recv, 1, y_sem)

        @pl.when(second_core & has_after)
        def _():
            take(2, 0, z_recv, 1, z_sem)

        round_grads(2, 0)
        middle_given.start()

    def own_head(x):
        lower_tile(0, 0, x, True)
        finish_query(x)
        return_query(x, 1)

    over_heads(own_head)

    for part, ref, factor in ((0, dk_ref, scale), (1, dv_ref, 1.0)):

        @pl.when(first_core)
        def _():
            take(0, 0, core_recv, 0, core_sem, (part,))

        take(0, 0, y_recv, 0, y_sem, (part,))

        @pl.when(has_after)
        def _():
            take(0, 0, z_recv, 0, z_sem, (part,))

        dkv_send[part] = (acc_kv[0, 0, part] * factor).astype(jnp.bfloat16)
        gather_back(
            dkv_send.at[part],
            ref.at[:, columns(place * HD)],
            result_out_sem.at[1 + part],
            result_sem.at[1 + part],
        )

    def drain(away):
        arrived(kv_buf.at[0, 0, :, 0:away, :], kv_in_out_sem.at[0])
        arrived(qd_buf.at[0, 0:away, :], q_out_sem.at[0])
        arrived(qd_buf.at[1, 0 : away - rows, :], q_out_sem.at[1])
        arrived(stat_recv.at[0 : away // rows], stat_sem.at[0])

    @pl.when(stays)
    def _():
        drain(unit - rows)

    @pl.when(jnp.logical_not(stays))
    def _():
        drain(unit)

    for index, (x, end) in enumerate(batches):
        arrived(relay_buf.at[:, x * HD : end * HD], relay_sem.at[2, index])
        to_between[index].wait_send()
    own_to_side.wait_send()
    own_side_given.wait_send()

    @pl.when(has_after)
    def _():
        own_to_after.wait_send()

    @pl.when(first_core)
    def _():
        own_to_core.wait_send()
        side_to_core.wait_send()

    @pl.when(has_before)
    def _():
        before_to_side.wait_send()
        before_to_core.wait_send()
        before_side_to_core.wait_send()
        middle_given.wait_send()
        middle_side_given.wait_send()

    @pl.when(second_core & has_before & has_after)
    def _():
        before_to_after.wait_send()

    @pl.when(has(1))
    def _():
        near_given.wait_send()
        near_side_given.wait_send()

    @pl.when(has(3))
    def _():
        far_given.wait_send()
        far_side_given.wait_send()

        @pl.when(first_core)
        def _():
            far_to_side.wait_send()

    def drain_back(away):
        arrived(dq_send.at[0:away, :], result_out_sem.at[0])
        for part in range(2):
            arrived(dkv_send.at[part, 0:away, :], result_out_sem.at[1 + part])

    @pl.when(stays)
    def _():
        drain_back(unit - rows)

    @pl.when(jnp.logical_not(stays))
    def _():
        drain_back(unit)

    for index, ref in enumerate((dq_ref, dk_ref, dv_ref)):
        arrived(ref, result_sem.at[index])


def hand_over(dq_in, dk_in, dv_in, dq_out, dk_out, dv_out, dq_vm, dk_vm, dv_vm, sems):
    ways = ((dk_in, dk_vm, dk_out), (dv_in, dv_vm, dv_out), (dq_in, dq_vm, dq_out))
    ins = [pltpu.make_async_copy(src, vm, sems.at[0, i]) for i, (src, vm, dst) in enumerate(ways)]
    outs = [pltpu.make_async_copy(vm, dst, sems.at[1, i]) for i, (src, vm, dst) in enumerate(ways)]
    for copy in ins:
        copy.start()
    for first, second in zip(ins, outs):
        first.wait()
        second.start()
    for copy in outs:
        copy.wait()


def body(queries, keys, values, attn_out, grad_out, log_norm, doc_lengths):
    heads = lax.axis_size("head")
    planes = lax.axis_size("ctx") // ROW
    rows = queries.shape[0]
    unit = rows * heads
    group = queries.shape[1] // keys.shape[1]
    low, full = jnp.bfloat16, jnp.float32
    anywhere = pl.BlockSpec(memory_space=pl.ANY)
    pairs = unit * unit * 6.5 * group
    dma = pltpu.SemaphoreType.DMA
    results = (
        jax.ShapeDtypeStruct(queries.shape, low),
        jax.ShapeDtypeStruct(keys.shape, low),
        jax.ShapeDtypeStruct(values.shape, low),
    )
    gradients = pl.pallas_call(
        functools.partial(kernel, planes, group),
        out_shape=results,
        in_specs=[pl.BlockSpec(memory_space=pltpu.SMEM)]
        + [anywhere] * 5
        + [pl.BlockSpec(memory_space=pltpu.VMEM)],
        out_specs=(anywhere, anywhere, anywhere),
        scratch_shapes=[
            pltpu.VMEM(attn_out.shape, low),
            pltpu.VMEM(grad_out.shape, low),
            pltpu.VMEM((2, unit, group * HD), low),
            pltpu.VMEM((rows, group * HD), low),
            pltpu.VMEM((group, 2, 2 * HD, unit), low),
            pltpu.VMEM((BACK + 1, 2, 2, unit, HD), low),
            pltpu.VMEM((BACK + 1, 2, HD, unit), low),
            pltpu.VMEM((ROW, 16, rows), full),
            pltpu.VMEM((4, 16, rows), full),
            pltpu.VMEM((HD, unit), full),
            pltpu.VMEM((BACK + 1, 2, unit, HD), low),
            pltpu.VMEM((BACK + 1, 2, 2, unit, HD), full),
            pltpu.VMEM((group, HD, unit), full),
            pltpu.VMEM((BACK + 1, 2, 2, unit, HD), low),
            pltpu.VMEM((4, 2, unit, HD), low),
            pltpu.VMEM((3, 2, unit, HD), low),
            pltpu.VMEM((2, 2, unit, HD), low),
            pltpu.VMEM((unit, group * HD), low),
            pltpu.VMEM((2, unit, HD), low),
            dma((2,)),
            dma((2,)),
            dma((2,)),
            dma((3, 2)),
            dma((BACK + 1, 2, 2)),
            dma((1,)),
            dma((9,)),
            dma((2,)),
            dma((4, 2)),
            dma((3, 2)),
            dma((2, 2)),
            dma((BACK + 1, 2)),
            dma((3,)),
            dma((3,)),
        ],
        compiler_params=pltpu.CompilerParams(
            collective_id=0, has_side_effects=True, vmem_limit_bytes=63 * 1024 * 1024
        ),
        cost_estimate=pl.CostEstimate(
            flops=int(10 * pairs * HD), bytes_accessed=8 * 1024 * 1024, transcendentals=int(pairs)
        ),
    )(doc_lengths, queries, keys, values, attn_out, grad_out, log_norm)
    return pl.pallas_call(
        hand_over,
        out_shape=results,
        in_specs=[anywhere] * 3,
        out_specs=(anywhere,) * 3,
        scratch_shapes=[pltpu.VMEM(result.shape, low) for result in results] + [dma((2, 3))],
        compiler_params=pltpu.CompilerParams(vmem_limit_bytes=63 * 1024 * 1024),
        cost_estimate=pl.CostEstimate(flops=0, bytes_accessed=2 * 1024 * 1024, transcendentals=0),
    )(*gradients)


def solution(mesh):
    spread = P(("ctx", "head"), None)
    return jax.shard_map(
        body,
        mesh=mesh,
        in_specs=(spread, spread, spread, spread, spread, P(None, ("ctx", "head")), P()),
        out_specs=(spread, spread, spread),
        check_vma=False,
    )
```
